512 devices in a mesh: fsdp: 16 (over y, z_hi, core), seq: 32 (over x, z_lo).
Axes of the slice: x: 4, y: 4, z: 16 (z_hi: 2, z_lo: 8; z = z_hi * 8 + z_lo), core: 2. Of those that a mesh axis runs over, the one named last changes fastest.
Arguments:
- query_raw: bfloat16 [16, 4096, 4096], P('fsdp', 'seq'), may hold values from -450 to 450, as said below
- out_cotangent: bfloat16 [16, 4096, 4096], P('fsdp', 'seq'), may hold values from -72 to 72, as said below
- text_keys: bfloat16 [16, 512, 4096], P('fsdp', 'seq'), may hold values from -450 to 450, as said below
- text_values: bfloat16 [16, 512, 4096], P('fsdp', 'seq'), may hold values from -24 to 24
- text_lengths: int32 [16], P('fsdp'), may hold values from 256 to 512
- gain_query: float32 [4096], P('fsdp'), may hold values from 0.1 to 1.9
- gain_key: float32 [4096], P('fsdp'), may hold values from 0.1 to 1.9
Outputs:
- attention_out: bfloat16 [16, 4096, 4096], P('fsdp', 'seq')
- query_grad: bfloat16 [16, 4096, 4096], P('fsdp', 'seq')
- gain_grad: float32 [4096], P('fsdp')
The draws below stay inside these ranges and needn't reach their ends.
Inputs may be any that keep to these rules, and one draw needn't show every extreme that they name: `query_raw`: finite values. `text_keys`: finite values. `out_cotangent`: finite values.
All inputs are finite; a program needn't handle non-finite values.
Results may differ from the reference program's by a relative error of at most 0.034.
Values may be sent and summed in bfloat16 or wider, within the bound.
A program may use at most 64 MiB of HBM per device.

```python
import math
import jax
import jax.numpy as jnp
from jax import lax

HEADS = 32
DH = 128
TEXT = 512
WIDTH = 4096
TOKENS = 4096
CLIPS = 16


def column_scales(key):
    return jnp.exp(jax.random.uniform(jax.random.fold_in(key, 101), (HEADS * DH,), jnp.float32, 0.0, math.log(10.0)))


def text_matrix(key, columns, off_level, mixing, jitter):
    feature_count = HEADS * DH
    normals = jnp.clip(jax.random.normal(jax.random.fold_in(key, 102), (CLIPS, TEXT, feature_count), jnp.float32), -4.0, 4.0)
    row_scales = jnp.exp(jax.random.uniform(jax.random.fold_in(key, 103), (CLIPS, TEXT, 1), jnp.float32, 0.0, math.log(10.0)))
    position = jnp.arange(TEXT)
    pair_index = position // 2
    in_pair = position < 2 * HEADS
    odd_rows = jnp.logical_and(in_pair, position % 2 == 1)
    column_head = jnp.arange(feature_count) // DH
    in_head = (column_head[None, :] == pair_index[:, None]).astype(jnp.float32)
    blended = jnp.where(odd_rows[:, None], (1.0 + mixing * jitter * in_head) * normals, normals)
    off_scale = off_level ** (1.0 + (pair_index % 3).astype(jnp.float32))
    damping = jnp.where(jnp.logical_and(in_pair[:, None], in_head == 0.0), off_scale[:, None], 1.0)
    return blended * damping * row_scales * columns


def draw_text_keys(key, part):
    columns = column_scales(key)
    result = text_matrix(key, columns, 1.0, 0.0, 0.0)
    return result.astype(jnp.bfloat16)


def draw_query_raw(key, part):
    columns = column_scales(key)
    own_key = jax.random.fold_in(key, 7)
    feature_count = HEADS * DH
    normals = jnp.clip(jax.random.normal(jax.random.fold_in(own_key, 1), (CLIPS, TOKENS, feature_count), jnp.float32), -4.0, 4.0)
    row_scales = jnp.exp(jax.random.uniform(jax.random.fold_in(own_key, 2), (CLIPS, TOKENS, 1), jnp.float32, 0.0, math.log(10.0)))
    result = normals * row_scales * columns
    return result.astype(jnp.bfloat16)


def draw_out_cotangent(key, part):
    own_key = jax.random.fold_in(key, 11)
    feature_count = HEADS * DH
    clip_rise = 1.0 + 2.0 * jnp.arange(CLIPS).astype(jnp.float32) / max(CLIPS - 1, 1)
    token_rise = 1.0 + 2.0 * jnp.arange(TOKENS).astype(jnp.float32) / max(TOKENS - 1, 1)
    rising = clip_rise[:, None, None] * token_rise[None, :, None]
    normals = jnp.clip(jax.random.normal(jax.random.fold_in(own_key, 1), (CLIPS, TOKENS, feature_count), jnp.float32), -4.0, 4.0)
    result = normals * rising
    return result.astype(jnp.bfloat16)


def touch_ends(values, stream_key, least, largest):
    index_at = [jax.random.randint(jax.random.fold_in(stream_key, axis), (), 0, length) for axis, length in enumerate(values.shape)]
    widest = values.shape.index(max(values.shape))
    beside = index_at[:widest] + [(index_at[widest] + 1) % values.shape[widest]] + index_at[widest + 1:]
    return values.at[tuple(index_at)].set(least).at[tuple(beside)].set(largest)


def level_of(key, extent, split, smallest, largest):
    factor_of, own = 1.0, jax.random.fold_in(key, 6)
    for dim, shards_of in split:
        steps = jnp.exp(jax.random.uniform(jax.random.fold_in(own, dim), (shards_of,), jnp.float32, smallest / len(split), largest / len(split)))
        factor_of = factor_of * jnp.repeat(steps, extent[dim] // shards_of).reshape([-1 if axis == dim else 1 for axis in range(len(extent))])
    return factor_of


def normal_values(key, extent, deviation, reach, shards=(), held_as=jnp.bfloat16):
    values = deviation * jax.random.normal(key, extent, jnp.float32)
    if shards:
        values = values * level_of(key, extent, shards, -0.22, 0.18)
    return jnp.clip(values, -reach, reach).astype(held_as)


def setup_inputs(seed: int = 0) -> dict:
    streams_of = jax.random.split(jax.random.key(seed), 8)
    return {
        "query_raw": draw_query_raw(jax.random.fold_in(streams_of[7], 71), 0),
        "out_cotangent": draw_out_cotangent(jax.random.fold_in(streams_of[7], 71), 0),
        "text_keys": draw_text_keys(jax.random.fold_in(streams_of[7], 71), 0),
        "text_values": normal_values(streams_of[3], (CLIPS, TEXT, WIDTH), 4.0, 24.0, ((0, 16), (1, 32))),
        "text_lengths": touch_ends(jax.random.randint(streams_of[4], (CLIPS,), TEXT // 2, TEXT + 1), jax.random.fold_in(streams_of[4], 1), TEXT // 2, TEXT).astype(jnp.int32),
        "gain_query": jnp.clip(1.0 + 0.18 * jax.random.normal(streams_of[5], (WIDTH,), jnp.float32), 0.1, 1.9),
        "gain_key": jnp.clip(1.0 + 0.18 * jax.random.normal(streams_of[6], (WIDTH,), jnp.float32), 0.1, 1.9),
    }


epsilon = 1e-06
masked_value = -1e+30

def unit_rows(entries):
    inverse = lax.rsqrt(lax.optimization_barrier(jnp.mean(entries * entries, axis=-1, keepdims=True)) + epsilon)
    return (inverse, entries * inverse)

def reference(query_raw, out_cotangent, text_keys, text_values, text_lengths, gain_query, gain_key):
    score_scale = DH ** (-0.5)

    def one_clip(packed):
        query_rows, cotangent, key_rows, value_rows, length = packed
        inverse, q_unit = unit_rows(query_rows.astype(jnp.float32))
        q_norm = (q_unit * gain_query * score_scale).astype(jnp.bfloat16)
        k_unit = unit_rows(key_rows.astype(jnp.float32))[1]
        k_norm = (k_unit * gain_key).astype(jnp.bfloat16)
        q_heads = q_norm.reshape(TOKENS, HEADS, DH).astype(jnp.float32)
        k_heads = k_norm.reshape(TEXT, HEADS, DH).astype(jnp.float32)
        v_heads = value_rows.reshape(TEXT, HEADS, DH).astype(jnp.float32)
        g_heads = cotangent.reshape(TOKENS, HEADS, DH).astype(jnp.float32)
        usable = jnp.arange(TEXT) < length
        scores = jnp.einsum('thd,jhd->htj', q_heads, k_heads)
        scores = jnp.where(usable[None, None, :], scores, masked_value)
        row_max = lax.optimization_barrier(jnp.max(scores, axis=-1, keepdims=True))
        exponent_terms = jnp.exp(scores - row_max)
        softmax = exponent_terms / lax.optimization_barrier(jnp.sum(exponent_terms, axis=-1, keepdims=True))
        softmax_low = lax.optimization_barrier(softmax.astype(jnp.bfloat16)).astype(jnp.float32)
        attention = jnp.einsum('htj,jhd->thd', softmax_low, v_heads).astype(jnp.bfloat16)
        row_delta = lax.optimization_barrier(jnp.sum(g_heads * attention.astype(jnp.float32), axis=-1))
        prob_grad = jnp.einsum('thd,jhd->htj', g_heads, v_heads)
        score_grad = (softmax * (prob_grad - jnp.transpose(row_delta)[:, :, None])).astype(jnp.bfloat16)
        score_float = lax.optimization_barrier(score_grad).astype(jnp.float32)
        dq_norm = jnp.einsum('htj,jhd->thd', score_float, k_heads).astype(jnp.bfloat16)
        dq_float = dq_norm.reshape(TOKENS, HEADS * DH).astype(jnp.float32)
        dq_unit = dq_float * gain_query * score_scale
        query_grad = (inverse * (dq_unit - q_unit * lax.optimization_barrier(jnp.mean(dq_unit * q_unit, axis=-1, keepdims=True)))).astype(jnp.bfloat16)
        gain_part = lax.optimization_barrier(jnp.sum(dq_float * q_unit, axis=0)) * score_scale
        return (attention.reshape(TOKENS, HEADS * DH), query_grad, gain_part)
    attention_out, query_grad, gain_parts = lax.map(one_clip, (query_raw, out_cotangent, text_keys, text_values, text_lengths))
    return (attention_out, query_grad, lax.optimization_barrier(jnp.sum(gain_parts, axis=0)))
```

```python
import functools

import jax
import jax.numpy as jnp
from jax import lax
from jax.experimental import pallas as pl
from jax.experimental.pallas import tpu as pltpu
from jax.sharding import PartitionSpec as P

MESH = pl.DeviceIdType.MESH
DH = 128
NX = 4
NL = 4
EPS = 1e-6
LOG2E = 1.4426950408889634
MASKED = -1e30
VMEM_LIMIT = 61 * 1024 * 1024
F32 = jnp.float32
BF16 = jnp.bfloat16


def attention_kernel(
    dims,
    len_ref,
    q_hbm,
    do_hbm,
    k_hbm,
    v_hbm,
    gq_ref,
    gk_ref,
    att,
    grad,
    gg_ref,
    kv,
    kv_send,
    kraw,
    vraw,
    q,
    qin,
    o_send,
    dqin,
    inv_row,
    inv,
    rowacc,
    gains,
    part,
    row_part,
    sum_y,
    sum_l,
    sum_x,
    sum_z,
    load_sem,
    own_sem,
    kvx_sem,
    z_recv,
    zu_send,
    zd_send,
    in_send,
    in_recv,
    o_send_sem,
    o_recv,
    dq_send_sem,
    dq_recv,
    inv_sem,
    gain_sem,
    sum_sem,
):
    nz, nf, heads, rows, text = dims
    ny = nf // NL
    own_heads = heads // NX
    depth = text // (NX * nz)
    groups = own_heads
    wx = own_heads * DH
    dev_heads = heads // nf
    f = lax.axis_index("fsdp")
    s = lax.axis_index("seq")
    x = s // nz
    z = s % nz
    y = f // NL
    low = f % NL

    def at_x(i):
        return (f, ((x + i) % NX) * nz + z)

    def at_z(i):
        return (f, x * nz + (z + i) % nz)

    def at_y(i):
        return (((y + i) % ny) * NL + low, s)

    def at_low(i):
        return (y * NL + (low + i) % NL, s)

    peers = (
        [at_x(i) for i in range(1, NX)]
        + [at_z(i) for i in range(1, nz)]
        + [at_y(i) for i in range(1, ny)]
        + [at_low(i) for i in range(1, NL)]
    )

    def remote(src, dst, send, recv, target):
        return pltpu.make_async_remote_copy(
            src_ref=src,
            dst_ref=dst,
            send_sem=send,
            recv_sem=recv,
            device_id=target,
            device_id_type=MESH,
        )

    load_k = pltpu.make_async_copy(k_hbm, kraw, load_sem.at[0])
    load_v = pltpu.make_async_copy(v_hbm, vraw, load_sem.at[1])
    load_q = pltpu.make_async_copy(q_hbm, q, load_sem.at[2])
    for load in (load_k, load_v, load_q):
        load.start()

    barrier = pltpu.get_barrier_semaphore()
    for peer in peers:
        pl.semaphore_signal(barrier, inc=1, device_id=peer, device_id_type=MESH)

    def columns(head):
        return pl.ds(pl.multiple_of(head * DH, DH), DH)

    @pl.loop(0, groups)
    def _(g):
        cols = columns(x * groups + g)
        pltpu.make_async_copy(q_hbm.at[:, cols], qin.at[g, x, 0], own_sem).start()
        pltpu.make_async_copy(do_hbm.at[:, cols], qin.at[g, x, 1], own_sem).start()

    for i in range(dev_heads):
        gains[dev_heads * f + i, 0:1] = gq_ref[i]
        gains[dev_heads * f + i, 1:2] = gk_ref[i]

    load_k.wait()
    load_v.wait()
    k32 = kraw[...].astype(F32)
    k_unit = k32 * lax.rsqrt(jnp.mean(k32 * k32, axis=-1, keepdims=True) + EPS)
    k_unit = k_unit.astype(BF16)
    for h in range(heads):
        kv_send[h // groups, h % groups, 0] = k_unit[:, h * DH : (h + 1) * DH]
        kv_send[h // groups, h % groups, 1] = vraw[:, h * DH : (h + 1) * DH]
    kv[:, z, x] = kv_send[x]

    load_q.wait()
    q32 = q[...].astype(F32)
    inv_col = lax.rsqrt(jnp.mean(q32 * q32, axis=-1, keepdims=True) + EPS)
    inv_wide = jnp.broadcast_to(inv_col, (rows, DH))
    inv[x] = inv_wide
    inv_row[x] = jnp.transpose(inv_wide)[0:1, :]
    rowacc[...] = jnp.zeros_like(rowacc)

    pl.semaphore_wait(barrier, len(peers))

    def kvx_copy(i):
        return remote(
            kv_send.at[(x + i) % NX], kv.at[:, z, x], kvx_sem.at[0], kvx_sem.at[1], at_x(i)
        )

    def inv_copy(i):
        return remote(inv_row.at[x], inv_row.at[x], inv_sem.at[0], inv_sem.at[1], at_x(i))

    def in_copies(g, i):
        cols = columns(((x + i) % NX) * groups + g)
        return (
            remote(q_hbm.at[:, cols], qin.at[g, x, 0], in_send, in_recv.at[g, x], at_x(i)),
            remote(do_hbm.at[:, cols], qin.at[g, x, 1], in_send, in_recv.at[g, x], at_x(i)),
        )

    def out_copies(g, i):
        head = x * groups + g
        to = (x + i) % NX
        return (
            remote(o_send.at[g, to, 0], att.at[:, columns(head)], o_send_sem, o_recv, at_x(i)),
            remote(o_send.at[g, to, 1], dqin.at[head], dq_send_sem, dq_recv.at[g], at_x(i)),
        )

    def z_copy(g, zz, up):
        chunk = kv.at[g, zz]
        send = zu_send if up else zd_send
        return remote(
            chunk, chunk, send.at[zz], z_recv.at[g, zz], at_z(1) if up else at_z(nz - 1)
        )

    def settle_recv(ref, sem):
        remote(ref, ref, sem, sem, at_x(1)).wait_recv()

    def settle_send(ref, sem):
        remote(ref, ref, sem, sem, at_x(1)).wait_send()

    for i in range(1, NX):
        kvx_copy(i).start()

    def in_sends(g):
        for i in range(1, NX):
            for copy in in_copies(g, i):
                copy.start()

    in_sends(0)
    for i in range(1, NX):
        inv_copy(i).start()

    block = gains.at[pl.ds(dev_heads * f, dev_heads)]
    for i in range(1, NL):
        remote(block, block, gain_sem.at[0], gain_sem.at[1], at_low(i)).start()

    index = lax.broadcasted_iota(jnp.int32, (1, text), 1)
    chunk_rows = NX * depth
    token = ((index // depth) % NX * nz + index // chunk_rows) * depth + index % depth
    bias = jnp.where(token < len_ref[0], 0.0, MASKED).astype(F32)
    scale = DH**-0.5
    nt = (((1,), (1,)), ((), ()))

    def compute(g):
        head = x * groups + g
        gain_q = gains[head, 0:1]
        gain_k = gains[head, 1:2]
        factor = gain_q * gain_k * (scale * LOG2E)
        keys = kv[g, :, :, 0].reshape(text, DH)
        values = kv[g, :, :, 1].reshape(text, DH)
        for i in (1, 2, 3, 0):
            source = (x + i) % NX
            q_low = (qin[g, source, 0].astype(F32) * inv[source] * factor).astype(BF16)
            cot = qin[g, source, 1]
            sc = lax.dot_general(q_low, keys, nt, preferred_element_type=F32) + bias
            e = jnp.exp2(sc - jnp.max(sc, axis=-1, keepdims=True))
            inv_sum = 1.0 / jnp.sum(e, axis=-1, keepdims=True)
            o = jnp.dot(e.astype(BF16), values, preferred_element_type=F32) * inv_sum
            o_low = o.astype(BF16)
            delta = jnp.sum(cot.astype(F32) * o_low.astype(F32), axis=-1, keepdims=True)
            dp = lax.dot_general(cot, values, nt, preferred_element_type=F32)
            ds = (e * (dp - delta)).astype(BF16)
            dq = jnp.dot(ds, keys, preferred_element_type=F32) * inv_sum * gain_k
            if i == 0:
                att[:, columns(head)] = o_low
                dqin[head] = dq.astype(BF16)
            else:
                o_send[g, source, 0] = o_low
                o_send[g, source, 1] = dq.astype(BF16)
                for copy in out_copies(g, i):
                    copy.start()

    def post(g):
        settle_recv(dqin.at[pl.ds(0, NX - 1)], dq_recv.at[g])
        for xx in range(NX):
            head = xx * groups + g
            q_unit = q[:, columns(head)].astype(F32) * inv[x]
            product = dqin[head].astype(F32) * q_unit
            rowacc[...] += product * (gains[head, 0:1] * scale)
            part[head] = jnp.sum(product, axis=0, keepdims=True) * scale

    last = nz - 1

    def step(n, carry):
        @pl.when(n == 0)
        def _():
            settle_recv(kv.at[:, z, 0 : NX - 1], kvx_sem.at[1])

        @pl.when(n < groups)
        def _():
            @pl.when(z < last)
            def _():
                z_copy(n, z, True).start()

            @pl.when(z > 0)
            def _():
                z_copy(n, z, False).start()

        @pl.loop(1, nz)
        def _(d):
            g = n - d
            live = jnp.logical_and(g >= 0, g < groups)

            @pl.when(jnp.logical_and(live, z - d >= 0))
            def _():
                z_copy(g, z - d, True).wait_recv()

                @pl.when(z < last)
                def _():
                    z_copy(g, z - d, True).start()

            @pl.when(jnp.logical_and(live, z + d < nz))
            def _():
                z_copy(g, z + d, False).wait_recv()

                @pl.when(z > 0)
                def _():
                    z_copy(g, z + d, False).start()

        @pl.when(n + 1 < groups)
        def _():
            in_sends(n + 1)

        @pl.when(n == min(1, last - 1))
        def _():
            settle_recv(gains.at[pl.ds(0, (NL - 1) * dev_heads)], gain_sem.at[1])
            row = gains.at[pl.ds(y * NL * dev_heads, NL * dev_heads)]
            for i in range(1, ny):
                remote(row, row, gain_sem.at[2], gain_sem.at[3], at_y(i)).start()

        @pl.when(n == min(2, last - 1))
        def _():
            if ny > 1:
                settle_recv(gains.at[pl.ds(0, (ny - 1) * NL * dev_heads)], gain_sem.at[3])
            settle_recv(inv_row.at[pl.ds(0, NX - 1)], inv_sem.at[1])
            for i in range(1, NX):
                source = (x + i) % NX
                wide = jnp.broadcast_to(inv_row[source], (DH, rows))
                inv[source] = jnp.transpose(wide)[:, 0:DH]
            pltpu.make_async_copy(qin.at[:, x], qin.at[:, x], own_sem).wait()

        done = n - last

        @pl.when(jnp.logical_and(done >= 0, done < groups))
        def _():
            for i in range(1, NX):
                source = (x + i) % NX
                settle_recv(qin.at[done, source], in_recv.at[done, source])
            compute(done)

        returned = done - 2

        @pl.when(jnp.logical_and(returned >= 0, returned < groups))
        def _():
            post(returned)

        return carry

    lax.fori_loop(0, groups + last + 2, step, 0)

    def final(first, count):
        @pl.loop(first, first + count)
        def _(head):
            dq_unit = dqin[head].astype(F32) * (gains[head, 0:1] * scale)
            result = inv[x] * dq_unit - q[:, columns(head)].astype(F32) * slope
            grad[:, columns(head)] = result.astype(BF16)

    for i in range(1, ny):
        to = (y + i) % ny
        remote(
            part.at[pl.ds(to * NL * dev_heads, NL * dev_heads)],
            sum_y.at[y],
            sum_sem.at[0],
            sum_sem.at[1],
            at_y(i),
        ).start()
    sum_y[y] = part[pl.ds(y * NL * dev_heads, NL * dev_heads)]
    row_mean = jnp.sum(rowacc[...], axis=-1, keepdims=True) * (1.0 / (heads * DH))
    slope = inv[x] * inv[x] * row_mean
    final(0, heads // 4)
    if ny > 1:
        settle_recv(sum_y.at[pl.ds(0, ny - 1)], sum_sem.at[1])
    total = sum_y[0]
    for i in range(1, ny):
        total = total + sum_y[i]
    row_part[...] = total
    for i in range(1, NL):
        to = (low + i) % NL
        remote(
            row_part.at[pl.ds(to * dev_heads, dev_heads)],
            sum_l.at[low],
            sum_sem.at[2],
            sum_sem.at[3],
            at_low(i),
        ).start()
    sum_l[low] = row_part[pl.ds(low * dev_heads, dev_heads)]
    final(heads // 4, heads // 4)
    settle_recv(sum_l.at[pl.ds(0, NL - 1)], sum_sem.at[3])
    total = sum_l[0]
    for i in range(1, NL):
        total = total + sum_l[i]
    sum_x[x] = total
    for i in range(1, NX):
        remote(sum_x.at[x], sum_x.at[x], sum_sem.at[4], sum_sem.at[5], at_x(i)).start()
    final(heads // 2, heads // 4)
    settle_recv(sum_x.at[pl.ds(0, NX - 1)], sum_sem.at[5])
    total = sum_x[0]
    for i in range(1, NX):
        total = total + sum_x[i]
    sum_z[z] = total
    for i in range(1, nz):
        remote(sum_z.at[z], sum_z.at[z], sum_sem.at[6], sum_sem.at[7], at_z(i)).start()
    final(3 * heads // 4, heads // 4)

    settle_recv(att.at[:, 0 : (NX - 1) * wx], o_recv)
    settle_send(kv_send.at[0 : NX - 1], kvx_sem.at[0])
    settle_send(qin.at[:, 0 : NX - 1], in_send)
    settle_send(o_send.at[:, 0 : NX - 1, 0], o_send_sem)
    settle_send(o_send.at[:, 0 : NX - 1, 1], dq_send_sem)
    settle_send(inv_row.at[pl.ds(0, NX - 1)], inv_sem.at[0])
    settle_send(gains.at[pl.ds(0, (NL - 1) * dev_heads)], gain_sem.at[0])
    if ny > 1:
        settle_send(gains.at[pl.ds(0, (ny - 1) * NL * dev_heads)], gain_sem.at[2])

    @pl.loop(0, nz)
    def _(zz):
        @pl.when(jnp.logical_and(z < last, zz <= z))
        def _():
            settle_send(kv.at[:, zz], zu_send.at[zz])

        @pl.when(jnp.logical_and(z > 0, zz >= z))
        def _():
            settle_send(kv.at[:, zz], zd_send.at[zz])

    if ny > 1:
        settle_send(sum_y.at[pl.ds(0, ny - 1)], sum_sem.at[0])
    settle_send(sum_l.at[pl.ds(0, NL - 1)], sum_sem.at[2])
    settle_send(sum_x.at[pl.ds(0, NX - 1)], sum_sem.at[4])
    settle_recv(sum_z.at[pl.ds(0, nz - 1)], sum_sem.at[7])
    total = sum_z[0]
    for i in range(1, nz):
        total = total + sum_z[i]
    gg_ref[...] = total
    settle_send(sum_z.at[pl.ds(0, nz - 1)], sum_sem.at[6])


def on_device(nz, nf, query_raw, out_cotangent, text_keys, text_values, text_lengths, gain_query, gain_key):
    rows, width = query_raw.shape[1:]
    depth = text_keys.shape[1]
    heads = width // DH
    text = depth * NX * nz
    own = heads // NX
    dev_heads = heads // nf
    ny = nf // NL
    dims = (nz, nf, heads, rows, text)
    any_space = pl.BlockSpec(memory_space=pl.ANY)
    vmem = pl.BlockSpec(memory_space=pltpu.VMEM)
    dma = pltpu.SemaphoreType.DMA
    attention, query_grad, gain_grad = pl.pallas_call(
        functools.partial(attention_kernel, dims),
        out_shape=(
            jax.ShapeDtypeStruct((rows, width), BF16),
            jax.ShapeDtypeStruct((rows, width), BF16),
            jax.ShapeDtypeStruct((dev_heads, 1, DH), F32),
        ),
        in_specs=[pl.BlockSpec(memory_space=pltpu.SMEM)] + [any_space] * 4 + [vmem] * 2,
        out_specs=(vmem, vmem, vmem),
        scratch_shapes=[
            pltpu.VMEM((own, nz, NX, 2, depth, DH), BF16),
            pltpu.VMEM((NX, own, 2, depth, DH), BF16),
            pltpu.VMEM((depth, width), BF16),
            pltpu.VMEM((depth, width), BF16),
            pltpu.VMEM((rows, width), BF16),
            pltpu.VMEM((own, NX, 2, rows, DH), BF16),
            pltpu.VMEM((own, NX, 2, rows, DH), BF16),
            pltpu.VMEM((heads, rows, DH), BF16),
            pltpu.VMEM((NX, 1, rows), F32),
            pltpu.VMEM((NX, rows, DH), F32),
            pltpu.VMEM((rows, DH), F32),
            pltpu.VMEM((heads, 2, DH), F32),
            pltpu.VMEM((heads, 1, DH), F32),
            pltpu.VMEM((NL * dev_heads, 1, DH), F32),
            pltpu.VMEM((ny, NL * dev_heads, 1, DH), F32),
            pltpu.VMEM((NL, dev_heads, 1, DH), F32),
            pltpu.VMEM((NX, dev_heads, 1, DH), F32),
            pltpu.VMEM((nz, dev_heads, 1, DH), F32),
            dma((3,)),
            dma,
            dma((2,)),
            dma((own, nz)),
            dma((nz,)),
            dma((nz,)),
            dma,
            dma((own, NX)),
            dma,
            dma,
            dma,
            dma((own,)),
            dma((2,)),
            dma((4,)),
            dma((8,)),
        ],
        compiler_params=pltpu.CompilerParams(
            collective_id=0, has_side_effects=True, vmem_limit_bytes=VMEM_LIMIT
        ),
    )(
        text_lengths,
        query_raw[0],
        out_cotangent[0],
        text_keys[0],
        text_values[0],
        gain_query.reshape(dev_heads, 1, DH),
        gain_key.reshape(dev_heads, 1, DH),
    )
    return attention[None], query_grad[None], gain_grad.reshape(dev_heads * DH)


def solution(mesh):
    nf, ns = mesh.shape["fsdp"], mesh.shape["seq"]
    tokens = P("fsdp", "seq", None)
    return jax.shard_map(
        functools.partial(on_device, ns // NX, nf),
        mesh=mesh,
        in_specs=(tokens, tokens, tokens, tokens, P("fsdp"), P("fsdp"), P("fsdp")),
        out_specs=(tokens, tokens, P("fsdp")),
        check_vma=False,
    )
```

```python
import functools

import jax
import jax.numpy as jnp
from jax import lax
from jax.experimental import pallas as pl
from jax.experimental.pallas import tpu as pltpu
from jax.sharding import PartitionSpec as P

MESH = pl.DeviceIdType.MESH
DH = 128
NX = 4
NL = 4
EPS = 1e-6
LOG2E = 1.4426950408889634
MASKED = -1e30
VMEM_LIMIT = 61 * 1024 * 1024
F32 = jnp.float32
BF16 = jnp.bfloat16


def attention_kernel(
    dims,
    len_ref,
    q_hbm,
    do_hbm,
    k_hbm,
    v_hbm,
    gq_ref,
    gk_ref,
    att,
    grad,
    gg_ref,
    kv,
    kv_send,
    kraw,
    vraw,
    q,
    qin,
    o_send,
    dqin,
    inv_row,
    inv,
    rowacc,
    own_gains,
    gains,
    part,
    core_part,
    sum_c,
    sum_y,
    z_part,
    sum_z,
    load_sem,
    own_sem,
    kvx_sem,
    z_recv,
    zu_send,
    zd_send,
    in_send,
    in_recv,
    o_send_sem,
    o_recv,
    dq_send_sem,
    dq_recv,
    inv_sem,
    gain_sem,
    sum_sem,
):
    nz, nf, heads, rows, text = dims
    ny = nf // NL
    own_heads = heads // NX
    depth = text // (NX * nz)
    groups = own_heads
    wx = own_heads * DH
    dev_heads = heads // nf
    f = lax.axis_index("fsdp")
    s = lax.axis_index("seq")
    x = s // nz
    z = s % nz
    y = f // NL
    low = f % NL

    def at_x(i):
        return (f, ((x + i) % NX) * nz + z)

    def at_z(i):
        return (f, x * nz + (z + i) % nz)

    core = low % 2
    half = low // 2
    other_core = (y * NL + half * 2 + 1 - core, s)
    other_half = (y * NL + (1 - half) * 2 + core, s)
    place = half * nz + z
    places = NL // 2 * nz

    def at_place(i):
        to = (place + i) % places
        return (y * NL + to // nz * 2 + core, x * nz + to % nz)

    owner_row = x * NL + low

    barrier = pltpu.get_barrier_semaphore()

    def greet(peer):
        pl.semaphore_signal(barrier, inc=1, device_id=peer, device_id_type=MESH)

    def remote(src, dst, send, recv, target):
        return pltpu.make_async_remote_copy(
            src_ref=src,
            dst_ref=dst,
            send_sem=send,
            recv_sem=recv,
            device_id=target,
            device_id_type=MESH,
        )

    load_k = pltpu.make_async_copy(k_hbm, kraw, load_sem.at[0])
    load_v = pltpu.make_async_copy(v_hbm, vraw, load_sem.at[1])
    load_q = pltpu.make_async_copy(q_hbm, q, load_sem.at[2])
    for load in (load_k, load_v, load_q):
        load.start()

    @pl.loop(1, places)
    def _(i):
        greet(at_place(i))

    for i in range(1, NX):
        greet(at_x(i))
    greet(other_core)
    for i in range(ny):
        if i == 0:

            @pl.when(x != y)
            def _():
                greet((f, y * nz + z))

        else:
            greet((((y + i) % ny) * NL + low, y * nz + z))

    def columns(head):
        return pl.ds(pl.multiple_of(head * DH, DH), DH)

    for i in range(dev_heads):
        own_gains[i, 0:1] = gq_ref[i]
        own_gains[i, 1:2] = gk_ref[i]

    load_k.wait()
    load_v.wait()
    k32 = kraw[...].astype(F32)
    k_unit = k32 * lax.rsqrt(jnp.mean(k32 * k32, axis=-1, keepdims=True) + EPS)
    k_unit = k_unit.astype(BF16)
    for h in range(heads):
        kv_send[h // groups, h % groups, 0] = k_unit[:, h * DH : (h + 1) * DH]
        kv_send[h // groups, h % groups, 1] = vraw[:, h * DH : (h + 1) * DH]
    kv[:, z, x] = kv_send[x]

    load_q.wait()
    q32 = q[...].astype(F32)
    inv_col = lax.rsqrt(jnp.mean(q32 * q32, axis=-1, keepdims=True) + EPS)
    inv_wide = jnp.broadcast_to(inv_col, (rows, DH))
    inv[x] = inv_wide
    inv_row[x] = jnp.transpose(inv_wide)[0:1, :]
    rowacc[...] = jnp.zeros_like(rowacc)

    near = places - 1 + NX - 1 + 1 + ny - 1

    @pl.when(x == y)
    def _():
        pl.semaphore_wait(barrier, near)

    @pl.when(x != y)
    def _():
        pl.semaphore_wait(barrier, near + 1)

    def kvx_copy(i):
        return remote(
            kv_send.at[(x + i) % NX], kv.at[:, z, x], kvx_sem.at[0], kvx_sem.at[1], at_x(i)
        )

    def inv_copy(i):
        return remote(inv_row.at[x], inv_row.at[x], inv_sem.at[0], inv_sem.at[1], at_x(i))

    def in_copies(g, i):
        cols = columns(((x + i) % NX) * groups + g)
        return (
            remote(q_hbm.at[:, cols], qin.at[g, x, 0], in_send, in_recv.at[g, x], at_x(i)),
            remote(do_hbm.at[:, cols], qin.at[g, x, 1], in_send, in_recv.at[g, x], at_x(i)),
        )

    def out_copies(g, i):
        head = x * groups + g
        to = (x + i) % NX
        return (
            remote(o_send.at[g, to, 0], att.at[:, columns(head)], o_send_sem, o_recv, at_x(i)),
            remote(o_send.at[g, to, 1], dqin.at[head], dq_send_sem, dq_recv.at[g], at_x(i)),
        )

    def z_copy(g, zz, up):
        chunk = kv.at[g, zz]
        send = zu_send if up else zd_send
        return remote(
            chunk, chunk, send.at[zz], z_recv.at[g, zz], at_z(1) if up else at_z(nz - 1)
        )

    def settle_recv(ref, sem):
        remote(ref, ref, sem, sem, at_x(1)).wait_recv()

    def settle_send(ref, sem):
        remote(ref, ref, sem, sem, at_x(1)).wait_send()

    for i in range(1, NX):
        kvx_copy(i).start()

    def in_sends(g):
        for i in range(1, NX):
            for copy in in_copies(g, i):
                copy.start()

    in_sends(0)
    for i in range(1, NX):
        inv_copy(i).start()

    def gain_copy(src, first, count, stage, target):
        dst = gains.at[pl.ds(first, count)]
        return remote(
            dst if src is None else src, dst, gain_sem.at[stage], gain_sem.at[3 + stage], target
        )

    gain_turn = gain_copy(own_gains, low * dev_heads, dev_heads, 0, (owner_row, y * nz + z))
    gain_core = gain_copy(None, low * dev_heads, dev_heads, 1, other_core)
    gain_half = gain_copy(None, half * 2 * dev_heads, 2 * dev_heads, 2, other_half)

    @pl.when(x != y)
    def _():
        gain_turn.start()

    @pl.when(x == y)
    def _():
        gains[pl.ds(low * dev_heads, dev_heads)] = own_gains[...]

    in_sends(1)
    @pl.loop(0, groups)
    def _(g):
        cols = columns(x * groups + g)
        pltpu.make_async_copy(q_hbm.at[:, cols], qin.at[g, x, 0], own_sem).start()
        pltpu.make_async_copy(do_hbm.at[:, cols], qin.at[g, x, 1], own_sem).start()

    index = lax.broadcasted_iota(jnp.int32, (1, text), 1)
    chunk_rows = NX * depth
    token = ((index // depth) % NX * nz + index // chunk_rows) * depth + index % depth
    bias = jnp.where(token < len_ref[0], 0.0, MASKED).astype(F32)
    scale = DH**-0.5
    nt = (((1,), (1,)), ((), ()))

    def compute(g):
        head = x * groups + g
        gain_q = gains[g, 0:1]
        gain_k = gains[g, 1:2]
        factor = gain_q * gain_k * (scale * LOG2E)
        column = jnp.zeros((1, DH), F32)
        keys = kv[g, :, :, 0].reshape(text, DH)
        values = kv[g, :, :, 1].reshape(text, DH)
        for i in (1, 2, 3, 0):
            source = (x + i) % NX
            q_unit = qin[g, source, 0].astype(F32) * inv[source]
            q_low = (q_unit * factor).astype(BF16)
            cot = qin[g, source, 1]
            sc = lax.dot_general(q_low, keys, nt, preferred_element_type=F32) + bias
            e = jnp.exp2(sc - jnp.max(sc, axis=-1, keepdims=True))
            inv_sum = 1.0 / jnp.sum(e, axis=-1, keepdims=True)
            o = jnp.dot(e.astype(BF16), values, preferred_element_type=F32) * inv_sum
            o_low = o.astype(BF16)
            delta = jnp.sum(cot.astype(F32) * o_low.astype(F32), axis=-1, keepdims=True)
            dp = lax.dot_general(cot, values, nt, preferred_element_type=F32)
            ds = (e * (dp - delta)).astype(BF16)
            dq = jnp.dot(ds, keys, preferred_element_type=F32) * inv_sum * gain_k
            column = column + jnp.sum(dq * q_unit, axis=0, keepdims=True)
            dq = dq * (gain_q * scale)
            if i == 0:
                att[:, columns(head)] = o_low
                dqin[head] = dq.astype(BF16)
            else:
                o_send[g, source, 0] = o_low
                o_send[g, source, 1] = dq.astype(BF16)
                for copy in out_copies(g, i):
                    copy.start()
        gain_row = g // dev_heads
        part[(gain_row % 2 * 2 + gain_row // 2) * dev_heads + g % dev_heads] = column * scale

    def post(g):
        settle_recv(dqin.at[pl.ds(0, NX - 1)], dq_recv.at[g])
        for xx in range(NX):
            head = xx * groups + g
            q_unit = q[:, columns(head)].astype(F32) * inv[x]
            rowacc[...] += dqin[head].astype(F32) * q_unit

    last = nz - 1

    def step(n, carry):
        @pl.when(n == 0)
        def _():
            settle_recv(kv.at[:, z, 0 : NX - 1], kvx_sem.at[1])

        @pl.when(n < groups)
        def _():
            @pl.when(z < last)
            def _():
                z_copy(n, z, True).start()

            @pl.when(z > 0)
            def _():
                z_copy(n, z, False).start()

        @pl.loop(1, nz)
        def _(d):
            g = n - d
            live = jnp.logical_and(g >= 0, g < groups)

            @pl.when(jnp.logical_and(live, z - d >= 0))
            def _():
                z_copy(g, z - d, True).wait_recv()

                @pl.when(z < last)
                def _():
                    z_copy(g, z - d, True).start()

            @pl.when(jnp.logical_and(live, z + d < nz))
            def _():
                z_copy(g, z + d, False).wait_recv()

                @pl.when(z > 0)
                def _():
                    z_copy(g, z + d, False).start()

        @pl.when(n + 2 < groups)
        def _():
            in_sends(n + 2)

        @pl.when(n == min(2, last - 1))
        def _():
            @pl.when(x != y)
            def _():
                gain_turn.wait_recv()

            gain_core.start()
            settle_recv(inv_row.at[pl.ds(0, NX - 1)], inv_sem.at[1])
            for i in range(1, NX):
                source = (x + i) % NX
                wide = jnp.broadcast_to(inv_row[source], (DH, rows))
                inv[source] = jnp.transpose(wide)[:, 0:DH]
            pltpu.make_async_copy(qin.at[:, x], qin.at[:, x], own_sem).wait()

        @pl.when(n == min(3, last - 1))
        def _():
            gain_core.wait_recv()
            gain_half.start()

        @pl.when(n == last - 1)
        def _():
            gain_half.wait_recv()

        done = n - last

        @pl.when(jnp.logical_and(done >= 0, done < groups))
        def _():
            for i in range(1, NX):
                source = (x + i) % NX
                settle_recv(qin.at[done, source], in_recv.at[done, source])
            compute(done)

        returned = done - 2

        @pl.when(jnp.logical_and(returned >= 0, returned < groups))
        def _():
            post(returned)

        return carry

    lax.fori_loop(0, groups + last, step, 0)

    span = 2 * dev_heads
    to_core = remote(
        part.at[pl.ds((1 - core) * span, span)], sum_c, sum_sem.at[0], sum_sem.at[1], other_core
    )
    to_core.start()
    post(groups - 2)
    to_core.wait_recv()
    core_part[...] = part[pl.ds(core * span, span)] + sum_c[...]

    def to_row(i):
        return remote(
            core_part,
            sum_y.at[y],
            sum_sem.at[2],
            sum_sem.at[3],
            (owner_row, (x + i) % NX * nz + z),
        )

    for i in range(1, NX):
        to_row(i).start()

    @pl.when(x != y)
    def _():
        to_row(0).start()

    @pl.when(x == y)
    def _():
        sum_y[y] = core_part[...]

    @pl.when(x == y)
    def _():
        settle_recv(sum_y.at[pl.ds(0, ny - 1)], sum_sem.at[3])

    @pl.when(x != y)
    def _():
        settle_recv(sum_y.at[pl.ds(0, ny)], sum_sem.at[3])

    total = sum_y[0]
    for i in range(1, ny):
        total = total + sum_y[i]
    z_part[...] = total

    def to_place(i):
        to = (place + i) % places
        return remote(
            z_part.at[pl.ds(to // nz * dev_heads, dev_heads)],
            sum_z.at[place],
            sum_sem.at[4],
            sum_sem.at[5],
            at_place(i),
        )

    @pl.loop(0, places - 1)
    def _(i):
        to_place((i + places // 4) % (places - 1) + 1).start()

    sum_z[place] = z_part[pl.ds(half * dev_heads, dev_heads)]
    post(groups - 1)
    row_mean = jnp.sum(rowacc[...], axis=-1, keepdims=True) * (1.0 / (heads * DH))
    slope = inv[x] * inv[x] * row_mean

    @pl.loop(0, heads)
    def _(head):
        result = inv[x] * dqin[head].astype(F32) - q[:, columns(head)].astype(F32) * slope
        grad[:, columns(head)] = result.astype(BF16)

    settle_recv(att.at[:, 0 : (NX - 1) * wx], o_recv)
    settle_send(kv_send.at[0 : NX - 1], kvx_sem.at[0])
    settle_send(qin.at[:, 0 : NX - 1], in_send)
    settle_send(o_send.at[:, 0 : NX - 1, 0], o_send_sem)
    settle_send(o_send.at[:, 0 : NX - 1, 1], dq_send_sem)
    settle_send(inv_row.at[pl.ds(0, NX - 1)], inv_sem.at[0])
    gain_core.wait_send()
    gain_half.wait_send()
    to_core.wait_send()

    @pl.when(x == y)
    def _():
        settle_send(sum_y.at[pl.ds(0, NX - 1)], sum_sem.at[2])

    @pl.when(x != y)
    def _():
        gain_turn.wait_send()
        settle_send(sum_y.at[pl.ds(0, NX)], sum_sem.at[2])

    @pl.loop(0, nz)
    def _(zz):
        @pl.when(jnp.logical_and(z < last, zz <= z))
        def _():
            settle_send(kv.at[:, zz], zu_send.at[zz])

        @pl.when(jnp.logical_and(z > 0, zz >= z))
        def _():
            settle_send(kv.at[:, zz], zd_send.at[zz])

    settle_recv(sum_z.at[pl.ds(0, places - 1)], sum_sem.at[5])
    total = sum_z[0]
    for i in range(1, places):
        total = total + sum_z[i]
    gg_ref[...] = total
    settle_send(sum_z.at[pl.ds(0, places - 1)], sum_sem.at[4])


def on_device(nz, nf, query_raw, out_cotangent, text_keys, text_values, text_lengths, gain_query, gain_key):
    rows, width = query_raw.shape[1:]
    depth = text_keys.shape[1]
    heads = width // DH
    text = depth * NX * nz
    own = heads // NX
    dev_heads = heads // nf
    ny = nf // NL
    dims = (nz, nf, heads, rows, text)
    any_space = pl.BlockSpec(memory_space=pl.ANY)
    vmem = pl.BlockSpec(memory_space=pltpu.VMEM)
    dma = pltpu.SemaphoreType.DMA
    attention, query_grad, gain_grad = pl.pallas_call(
        functools.partial(attention_kernel, dims),
        out_shape=(
            jax.ShapeDtypeStruct((rows, width), BF16),
            jax.ShapeDtypeStruct((rows, width), BF16),
            jax.ShapeDtypeStruct((dev_heads, 1, DH), F32),
        ),
        in_specs=[pl.BlockSpec(memory_space=pltpu.SMEM)] + [any_space] * 4 + [vmem] * 2,
        out_specs=(vmem, vmem, vmem),
        scratch_shapes=[
            pltpu.VMEM((own, nz, NX, 2, depth, DH), BF16),
            pltpu.VMEM((NX, own, 2, depth, DH), BF16),
            pltpu.VMEM((depth, width), BF16),
            pltpu.VMEM((depth, width), BF16),
            pltpu.VMEM((rows, width), BF16),
            pltpu.VMEM((own, NX, 2, rows, DH), BF16),
            pltpu.VMEM((own, NX, 2, rows, DH), BF16),
            pltpu.VMEM((heads, rows, DH), BF16),
            pltpu.VMEM((NX, 1, rows), F32),
            pltpu.VMEM((NX, rows, DH), F32),
            pltpu.VMEM((rows, DH), F32),
            pltpu.VMEM((dev_heads, 2, DH), F32),
            pltpu.VMEM((own, 2, DH), F32),
            pltpu.VMEM((own, 1, DH), F32),
            pltpu.VMEM((own // 2, 1, DH), F32),
            pltpu.VMEM((own // 2, 1, DH), F32),
            pltpu.VMEM((ny, own // 2, 1, DH), F32),
            pltpu.VMEM((own // 2, 1, DH), F32),
            pltpu.VMEM((NL // 2 * nz, dev_heads, 1, DH), F32),
            dma((3,)),
            dma,
            dma((2,)),
            dma((own, nz)),
            dma((nz,)),
            dma((nz,)),
            dma,
            dma((own, NX)),
            dma,
            dma,
            dma,
            dma((own,)),
            dma((2,)),
            dma((6,)),
            dma((6,)),
        ],
        compiler_params=pltpu.CompilerParams(
            collective_id=0, has_side_effects=True, vmem_limit_bytes=VMEM_LIMIT
        ),
    )(
        text_lengths,
        query_raw[0],
        out_cotangent[0],
        text_keys[0],
        text_values[0],
        gain_query.reshape(dev_heads, 1, DH),
        gain_key.reshape(dev_heads, 1, DH),
    )
    return attention[None], query_grad[None], gain_grad.reshape(dev_heads * DH)


def solution(mesh):
    nf, ns = mesh.shape["fsdp"], mesh.shape["seq"]
    tokens = P("fsdp", "seq", None)
    return jax.shard_map(
        functools.partial(on_device, ns // NX, nf),
        mesh=mesh,
        in_specs=(tokens, tokens, tokens, tokens, P("fsdp"), P("fsdp"), P("fsdp")),
        out_specs=(tokens, tokens, P("fsdp")),
        check_vma=False,
    )
```

```python
import functools

import jax
import jax.numpy as jnp
from jax import lax
from jax.experimental import pallas as pl
from jax.experimental.pallas import tpu as pltpu
from jax.sharding import PartitionSpec as P

MESH = pl.DeviceIdType.MESH
DH = 128
NX = 4
NL = 4
AHEAD = 2
EPS = 1e-6
LOG2E = 1.4426950408889634
MASKED = -1e30
VMEM_LIMIT = 61 * 1024 * 1024
F32 = jnp.float32
BF16 = jnp.bfloat16


def attention_kernel(
    dims,
    len_ref,
    q_hbm,
    do_hbm,
    k_hbm,
    v_hbm,
    gq_ref,
    gk_ref,
    att,
    grad,
    gg_ref,
    kv,
    kv_send,
    kraw,
    vraw,
    q,
    qin,
    o_send,
    dqin,
    inv_row,
    inv,
    rowacc,
    own_gains,
    gains,
    part,
    core_part,
    sum_c,
    sum_y,
    z_part,
    sum_z,
    load_sem,
    own_sem,
    kvx_sem,
    z_recv,
    zu_send,
    zd_send,
    in_send,
    in_recv,
    o_send_sem,
    o_recv,
    dq_send_sem,
    dq_recv,
    inv_sem,
    gain_sem,
    sum_sem,
):
    nz, nf, heads, rows, text = dims
    ny = nf // NL
    own_heads = heads // NX
    depth = text // (NX * nz)
    groups = own_heads
    wx = own_heads * DH
    dev_heads = heads // nf
    f = lax.axis_index("fsdp")
    s = lax.axis_index("seq")
    x = s // nz
    z = s % nz
    y = f // NL
    low = f % NL

    def at_x(i):
        return (f, ((x + i) % NX) * nz + z)

    def at_z(i):
        return (f, x * nz + (z + i) % nz)

    core = low % 2
    half = low // 2
    other_core = (y * NL + half * 2 + 1 - core, s)
    other_half = (y * NL + (1 - half) * 2 + core, s)
    place = half * nz + z
    places = NL // 2 * nz

    def at_place(i):
        to = (place + i) % places
        return (y * NL + to // nz * 2 + core, x * nz + to % nz)

    owner_row = x * NL + low

    barrier = pltpu.get_barrier_semaphore()

    def greet(peer):
        pl.semaphore_signal(barrier, inc=1, device_id=peer, device_id_type=MESH)

    def remote(src, dst, send, recv, target):
        return pltpu.make_async_remote_copy(
            src_ref=src,
            dst_ref=dst,
            send_sem=send,
            recv_sem=recv,
            device_id=target,
            device_id_type=MESH,
        )

    load_k = pltpu.make_async_copy(k_hbm, kraw, load_sem.at[0])
    load_v = pltpu.make_async_copy(v_hbm, vraw, load_sem.at[1])
    load_q = pltpu.make_async_copy(q_hbm, q, load_sem.at[2])
    for load in (load_k, load_v, load_q):
        load.start()

    @pl.loop(1, places)
    def _(i):
        greet(at_place(i))

    for i in range(1, NX):
        greet(at_x(i))
    greet(other_core)
    for i in range(ny):
        if i == 0:

            @pl.when(x != y)
            def _():
                greet((f, y * nz + z))

        else:
            greet((((y + i) % ny) * NL + low, y * nz + z))

    def columns(head):
        return pl.ds(pl.multiple_of(head * DH, DH), DH)

    for i in range(dev_heads):
        own_gains[i, 0:1] = gq_ref[i]
        own_gains[i, 1:2] = gk_ref[i]

    load_k.wait()
    load_v.wait()
    k32 = kraw[...].astype(F32)
    k_unit = k32 * lax.rsqrt(jnp.mean(k32 * k32, axis=-1, keepdims=True) + EPS)
    k_unit = k_unit.astype(BF16)
    for h in range(heads):
        kv_send[h // groups, h % groups, 0] = k_unit[:, h * DH : (h + 1) * DH]
        kv_send[h // groups, h % groups, 1] = vraw[:, h * DH : (h + 1) * DH]
    kv[:, z, x] = kv_send[x]

    load_q.wait()
    q32 = q[...].astype(F32)
    inv_col = lax.rsqrt(jnp.mean(q32 * q32, axis=-1, keepdims=True) + EPS)
    inv_wide = jnp.broadcast_to(inv_col, (rows, DH))
    inv[x] = inv_wide
    inv_row[x] = jnp.transpose(inv_wide)[0:1, :]
    rowacc[...] = jnp.zeros_like(rowacc)

    near = places - 1 + NX - 1 + 1 + ny - 1

    @pl.when(x == y)
    def _():
        pl.semaphore_wait(barrier, near)

    @pl.when(x != y)
    def _():
        pl.semaphore_wait(barrier, near + 1)

    def kvx_copy(i):
        return remote(
            kv_send.at[(x + i) % NX], kv.at[:, z, x], kvx_sem.at[0], kvx_sem.at[1], at_x(i)
        )

    def inv_copy(i):
        return remote(inv_row.at[x], inv_row.at[x], inv_sem.at[0], inv_sem.at[1], at_x(i))

    def in_copies(g, i):
        cols = columns(((x + i) % NX) * groups + g)
        return (
            remote(q_hbm.at[:, cols], qin.at[g, x, 0], in_send, in_recv.at[g, x], at_x(i)),
            remote(do_hbm.at[:, cols], qin.at[g, x, 1], in_send, in_recv.at[g, x], at_x(i)),
        )

    def out_copies(g, i):
        head = x * groups + g
        to = (x + i) % NX
        return (
            remote(o_send.at[g, to, 0], att.at[:, columns(head)], o_send_sem, o_recv, at_x(i)),
            remote(o_send.at[g, to, 1], dqin.at[head], dq_send_sem, dq_recv.at[g], at_x(i)),
        )

    def z_copy(g, zz, up):
        chunk = kv.at[g, zz]
        send = zu_send if up else zd_send
        return remote(
            chunk, chunk, send.at[zz], z_recv.at[g, zz], at_z(1) if up else at_z(nz - 1)
        )

    def settle_recv(ref, sem):
        remote(ref, ref, sem, sem, at_x(1)).wait_recv()

    def settle_send(ref, sem):
        remote(ref, ref, sem, sem, at_x(1)).wait_send()

    for i in range(1, NX):
        kvx_copy(i).start()

    def in_sends(g):
        for i in range(1, NX):
            for copy in in_copies(g, i):
                copy.start()

    in_sends(0)
    for i in range(1, NX):
        inv_copy(i).start()

    def gain_copy(src, first, count, stage, target):
        dst = gains.at[pl.ds(first, count)]
        return remote(
            dst if src is None else src, dst, gain_sem.at[stage], gain_sem.at[3 + stage], target
        )

    gain_turn = gain_copy(own_gains, low * dev_heads, dev_heads, 0, (owner_row, y * nz + z))
    gain_core = gain_copy(None, low * dev_heads, dev_heads, 1, other_core)
    gain_half = gain_copy(None, half * 2 * dev_heads, 2 * dev_heads, 2, other_half)

    @pl.when(x != y)
    def _():
        gain_turn.start()

    @pl.when(x == y)
    def _():
        gains[pl.ds(low * dev_heads, dev_heads)] = own_gains[...]

    in_sends(1)
    @pl.loop(0, groups)
    def _(g):
        cols = columns(x * groups + g)
        pltpu.make_async_copy(q_hbm.at[:, cols], qin.at[g, x, 0], own_sem).start()
        pltpu.make_async_copy(do_hbm.at[:, cols], qin.at[g, x, 1], own_sem).start()

    index = lax.broadcasted_iota(jnp.int32, (1, text), 1)
    chunk_rows = NX * depth
    token = ((index // depth) % NX * nz + index // chunk_rows) * depth + index % depth
    bias = jnp.where(token < len_ref[0], 0.0, MASKED).astype(F32)
    scale = DH**-0.5
    nt = (((1,), (1,)), ((), ()))

    def compute(g):
        head = x * groups + g
        gain_q = gains[g, 0:1]
        gain_k = gains[g, 1:2]
        factor = gain_q * gain_k * (scale * LOG2E)
        column = jnp.zeros((1, DH), F32)
        keys = kv[g, :, :, 0].reshape(text, DH)
        values = kv[g, :, :, 1].reshape(text, DH)
        for i in (1, 2, 3, 0):
            source = (x + i) % NX
            q_unit = qin[g, source, 0].astype(F32) * inv[source]
            q_low = (q_unit * factor).astype(BF16)
            cot = qin[g, source, 1]
            sc = lax.dot_general(q_low, keys, nt, preferred_element_type=F32) + bias
            e = jnp.exp2(sc - jnp.max(sc, axis=-1, keepdims=True))
            inv_sum = 1.0 / jnp.sum(e, axis=-1, keepdims=True)
            o = jnp.dot(e.astype(BF16), values, preferred_element_type=F32) * inv_sum
            o_low = o.astype(BF16)
            delta = jnp.sum(cot.astype(F32) * o_low.astype(F32), axis=-1, keepdims=True)
            dp = lax.dot_general(cot, values, nt, preferred_element_type=F32)
            ds = (e * (dp - delta)).astype(BF16)
            dq = jnp.dot(ds, keys, preferred_element_type=F32) * inv_sum * gain_k
            column = column + jnp.sum(dq * q_unit, axis=0, keepdims=True)
            dq = dq * (gain_q * scale)
            if i == 0:
                att[:, columns(head)] = o_low
                dqin[head] = dq.astype(BF16)
            else:
                o_send[g, source, 0] = o_low
                o_send[g, source, 1] = dq.astype(BF16)
                for copy in out_copies(g, i):
                    copy.start()
        gain_row = g // dev_heads
        part[(gain_row % 2 * 2 + gain_row // 2) * dev_heads + g % dev_heads] = column * scale

    def post(g):
        settle_recv(dqin.at[pl.ds(0, NX - 1)], dq_recv.at[g])
        for xx in range(NX):
            head = xx * groups + g
            q_unit = q[:, columns(head)].astype(F32) * inv[x]
            rowacc[...] += dqin[head].astype(F32) * q_unit

    last = nz - 1

    def own_sends(g):
        @pl.when(z < last)
        def _():
            z_copy(g, z, True).start()

        @pl.when(z > 0)
        def _():
            z_copy(g, z, False).start()

    def step(n, carry):
        @pl.when(n == 0)
        def _():
            settle_recv(kv.at[:, z, 0 : NX - 1], kvx_sem.at[1])

            for g in range(AHEAD):
                own_sends(g)

        @pl.when(n + AHEAD < groups)
        def _():
            own_sends(n + AHEAD)

        @pl.loop(1, nz)
        def _(d):
            g = n - d
            live = jnp.logical_and(g >= 0, g < groups)

            @pl.when(jnp.logical_and(live, z - d >= 0))
            def _():
                z_copy(g, z - d, True).wait_recv()

                @pl.when(z < last)
                def _():
                    z_copy(g, z - d, True).start()

            @pl.when(jnp.logical_and(live, z + d < nz))
            def _():
                z_copy(g, z + d, False).wait_recv()

                @pl.when(z > 0)
                def _():
                    z_copy(g, z + d, False).start()

        @pl.when(n + 2 < groups)
        def _():
            in_sends(n + 2)

        @pl.when(n == min(2, last - 1))
        def _():
            @pl.when(x != y)
            def _():
                gain_turn.wait_recv()

            gain_core.start()
            settle_recv(inv_row.at[pl.ds(0, NX - 1)], inv_sem.at[1])
            for i in range(1, NX):
                source = (x + i) % NX
                wide = jnp.broadcast_to(inv_row[source], (DH, rows))
                inv[source] = jnp.transpose(wide)[:, 0:DH]
            pltpu.make_async_copy(qin.at[:, x], qin.at[:, x], own_sem).wait()

        @pl.when(n == min(3, last - 1))
        def _():
            gain_core.wait_recv()
            gain_half.start()

        @pl.when(n == last - 1)
        def _():
            gain_half.wait_recv()

        done = n - last

        @pl.when(jnp.logical_and(done >= 0, done < groups))
        def _():
            for i in range(1, NX):
                source = (x + i) % NX
                settle_recv(qin.at[done, source], in_recv.at[done, source])
            compute(done)

        return carry

    lax.fori_loop(0, groups + last, step, 0)

    span = 2 * dev_heads
    to_core = remote(
        part.at[pl.ds((1 - core) * span, span)], sum_c, sum_sem.at[0], sum_sem.at[1], other_core
    )
    to_core.start()
    to_core.wait_recv()
    core_part[...] = part[pl.ds(core * span, span)] + sum_c[...]

    def to_row(i):
        return remote(
            core_part,
            sum_y.at[y],
            sum_sem.at[2],
            sum_sem.at[3],
            (owner_row, (x + i) % NX * nz + z),
        )

    for i in range(1, NX):
        to_row(i).start()

    @pl.when(x != y)
    def _():
        to_row(0).start()

    @pl.when(x == y)
    def _():
        sum_y[y] = core_part[...]

    @pl.loop(0, groups - 2)
    def _(g):
        post(g)

    @pl.when(x == y)
    def _():
        settle_recv(sum_y.at[pl.ds(0, ny - 1)], sum_sem.at[3])

    @pl.when(x != y)
    def _():
        settle_recv(sum_y.at[pl.ds(0, ny)], sum_sem.at[3])

    total = sum_y[0]
    for i in range(1, ny):
        total = total + sum_y[i]
    z_part[...] = total

    def to_place(i):
        to = (place + i) % places
        return remote(
            z_part.at[pl.ds(to // nz * dev_heads, dev_heads)],
            sum_z.at[place],
            sum_sem.at[4],
            sum_sem.at[5],
            at_place(i),
        )

    @pl.loop(0, places - 1)
    def _(i):
        to_place((i + places // 4) % (places - 1) + 1).start()

    sum_z[place] = z_part[pl.ds(half * dev_heads, dev_heads)]
    post(groups - 2)
    post(groups - 1)
    row_mean = jnp.sum(rowacc[...], axis=-1, keepdims=True) * (1.0 / (heads * DH))
    slope = inv[x] * inv[x] * row_mean

    @pl.loop(0, heads)
    def _(head):
        result = inv[x] * dqin[head].astype(F32) - q[:, columns(head)].astype(F32) * slope
        grad[:, columns(head)] = result.astype(BF16)

    settle_recv(att.at[:, 0 : (NX - 1) * wx], o_recv)
    settle_send(kv_send.at[0 : NX - 1], kvx_sem.at[0])
    settle_send(qin.at[:, 0 : NX - 1], in_send)
    settle_send(o_send.at[:, 0 : NX - 1, 0], o_send_sem)
    settle_send(o_send.at[:, 0 : NX - 1, 1], dq_send_sem)
    settle_send(inv_row.at[pl.ds(0, NX - 1)], inv_sem.at[0])
    gain_core.wait_send()
    gain_half.wait_send()
    to_core.wait_send()

    @pl.when(x == y)
    def _():
        settle_send(sum_y.at[pl.ds(0, NX - 1)], sum_sem.at[2])

    @pl.when(x != y)
    def _():
        gain_turn.wait_send()
        settle_send(sum_y.at[pl.ds(0, NX)], sum_sem.at[2])

    @pl.loop(0, nz)
    def _(zz):
        @pl.when(jnp.logical_and(z < last, zz <= z))
        def _():
            settle_send(kv.at[:, zz], zu_send.at[zz])

        @pl.when(jnp.logical_and(z > 0, zz >= z))
        def _():
            settle_send(kv.at[:, zz], zd_send.at[zz])

    settle_recv(sum_z.at[pl.ds(0, places - 1)], sum_sem.at[5])
    total = sum_z[0]
    for i in range(1, places):
        total = total + sum_z[i]
    gg_ref[...] = total
    settle_send(sum_z.at[pl.ds(0, places - 1)], sum_sem.at[4])


def on_device(nz, nf, query_raw, out_cotangent, text_keys, text_values, text_lengths, gain_query, gain_key):
    rows, width = query_raw.shape[1:]
    depth = text_keys.shape[1]
    heads = width // DH
    text = depth * NX * nz
    own = heads // NX
    dev_heads = heads // nf
    ny = nf // NL
    dims = (nz, nf, heads, rows, text)
    any_space = pl.BlockSpec(memory_space=pl.ANY)
    vmem = pl.BlockSpec(memory_space=pltpu.VMEM)
    dma = pltpu.SemaphoreType.DMA
    attention, query_grad, gain_grad = pl.pallas_call(
        functools.partial(attention_kernel, dims),
        out_shape=(
            jax.ShapeDtypeStruct((rows, width), BF16),
            jax.ShapeDtypeStruct((rows, width), BF16),
            jax.ShapeDtypeStruct((dev_heads, 1, DH), F32),
        ),
        in_specs=[pl.BlockSpec(memory_space=pltpu.SMEM)] + [any_space] * 4 + [vmem] * 2,
        out_specs=(vmem, vmem, vmem),
        scratch_shapes=[
            pltpu.VMEM((own, nz, NX, 2, depth, DH), BF16),
            pltpu.VMEM((NX, own, 2, depth, DH), BF16),
            pltpu.VMEM((depth, width), BF16),
            pltpu.VMEM((depth, width), BF16),
            pltpu.VMEM((rows, width), BF16),
            pltpu.VMEM((own, NX, 2, rows, DH), BF16),
            pltpu.VMEM((own, NX, 2, rows, DH), BF16),
            pltpu.VMEM((heads, rows, DH), BF16),
            pltpu.VMEM((NX, 1, rows), F32),
            pltpu.VMEM((NX, rows, DH), F32),
            pltpu.VMEM((rows, DH), F32),
            pltpu.VMEM((dev_heads, 2, DH), F32),
            pltpu.VMEM((own, 2, DH), F32),
            pltpu.VMEM((own, 1, DH), F32),
            pltpu.VMEM((own // 2, 1, DH), F32),
            pltpu.VMEM((own // 2, 1, DH), F32),
            pltpu.VMEM((ny, own // 2, 1, DH), F32),
            pltpu.VMEM((own // 2, 1, DH), F32),
            pltpu.VMEM((NL // 2 * nz, dev_heads, 1, DH), F32),
            dma((3,)),
            dma,
            dma((2,)),
            dma((own, nz)),
            dma((nz,)),
            dma((nz,)),
            dma,
            dma((own, NX)),
            dma,
            dma,
            dma,
            dma((own,)),
            dma((2,)),
            dma((6,)),
            dma((6,)),
        ],
        compiler_params=pltpu.CompilerParams(
            collective_id=0, has_side_effects=True, vmem_limit_bytes=VMEM_LIMIT
        ),
    )(
        text_lengths,
        query_raw[0],
        out_cotangent[0],
        text_keys[0],
        text_values[0],
        gain_query.reshape(dev_heads, 1, DH),
        gain_key.reshape(dev_heads, 1, DH),
    )
    return attention[None], query_grad[None], gain_grad.reshape(dev_heads * DH)


def solution(mesh):
    nf, ns = mesh.shape["fsdp"], mesh.shape["seq"]
    tokens = P("fsdp", "seq", None)
    return jax.shard_map(
        functools.partial(on_device, ns // NX, nf),
        mesh=mesh,
        in_specs=(tokens, tokens, tokens, tokens, P("fsdp"), P("fsdp"), P("fsdp")),
        out_specs=(tokens, tokens, P("fsdp")),
        check_vma=False,
    )
```

```python
import functools

import jax
import jax.numpy as jnp
from jax import lax
from jax.experimental import pallas as pl
from jax.experimental.pallas import tpu as pltpu
from jax.sharding import PartitionSpec as P

MESH = pl.DeviceIdType.MESH
DH = 128
NX = 4
NL = 4
AHEAD = 4
EPS = 1e-6
LOG2E = 1.4426950408889634
MASKED = -1e30
VMEM_LIMIT = 61 * 1024 * 1024
F32 = jnp.float32
BF16 = jnp.bfloat16


def attention_kernel(
    dims,
    len_ref,
    q_hbm,
    do_hbm,
    k_hbm,
    v_hbm,
    gq_ref,
    gk_ref,
    att,
    grad,
    gg_ref,
    kv,
    kv_send,
    kraw,
    vraw,
    q,
    qin,
    o_send,
    dqin,
    inv_row,
    inv,
    rowacc,
    own_gains,
    gains,
    part,
    core_part,
    sum_c,
    sum_y,
    z_part,
    sum_z,
    load_sem,
    own_sem,
    kvx_sem,
    z_recv,
    zu_send,
    zd_send,
    in_send,
    in_recv,
    o_send_sem,
    o_recv,
    dq_send_sem,
    dq_recv,
    inv_sem,
    gain_sem,
    sum_sem,
):
    nz, nf, heads, rows, text = dims
    ny = nf // NL
    own_heads = heads // NX
    depth = text // (NX * nz)
    groups = own_heads
    wx = own_heads * DH
    dev_heads = heads // nf
    f = lax.axis_index("fsdp")
    s = lax.axis_index("seq")
    x = s // nz
    z = s % nz
    y = f // NL
    low = f % NL

    def at_x(i):
        return (f, ((x + i) % NX) * nz + z)

    def at_z(i):
        return (f, x * nz + (z + i) % nz)

    core = low % 2
    half = low // 2
    other_core = (y * NL + half * 2 + 1 - core, s)
    other_half = (y * NL + (1 - half) * 2 + core, s)
    place = half * nz + z
    places = NL // 2 * nz

    def at_place(i):
        to = (place + i) % places
        return (y * NL + to // nz * 2 + core, x * nz + to % nz)

    owner_row = x * NL + low

    barrier = pltpu.get_barrier_semaphore()

    def greet(peer):
        pl.semaphore_signal(barrier, inc=1, device_id=peer, device_id_type=MESH)

    def remote(src, dst, send, recv, target):
        return pltpu.make_async_remote_copy(
            src_ref=src,
            dst_ref=dst,
            send_sem=send,
            recv_sem=recv,
            device_id=target,
            device_id_type=MESH,
        )

    load_k = pltpu.make_async_copy(k_hbm, kraw, load_sem.at[0])
    load_v = pltpu.make_async_copy(v_hbm, vraw, load_sem.at[1])
    load_q = pltpu.make_async_copy(q_hbm, q, load_sem.at[2])
    for load in (load_k, load_v, load_q):
        load.start()

    @pl.loop(1, places)
    def _(i):
        greet(at_place(i))

    for i in range(1, NX):
        greet(at_x(i))
    greet(other_core)
    for i in range(ny):
        if i == 0:

            @pl.when(x != y)
            def _():
                greet((f, y * nz + z))

        else:
            greet((((y + i) % ny) * NL + low, y * nz + z))

    def columns(head):
        return pl.ds(pl.multiple_of(head * DH, DH), DH)

    for i in range(dev_heads):
        own_gains[i, 0:1] = gq_ref[i]
        own_gains[i, 1:2] = gk_ref[i]

    load_k.wait()
    load_v.wait()
    k32 = kraw[...].astype(F32)
    k_unit = k32 * lax.rsqrt(jnp.mean(k32 * k32, axis=-1, keepdims=True) + EPS)
    k_unit = k_unit.astype(BF16)
    for h in range(heads):
        kv_send[h // groups, h % groups, 0] = k_unit[:, h * DH : (h + 1) * DH]
        kv_send[h // groups, h % groups, 1] = vraw[:, h * DH : (h + 1) * DH]
    kv[:, z, x] = kv_send[x]

    load_q.wait()
    q32 = q[...].astype(F32)
    inv_col = lax.rsqrt(jnp.mean(q32 * q32, axis=-1, keepdims=True) + EPS)
    inv_wide = jnp.broadcast_to(inv_col, (rows, DH))
    inv[x] = inv_wide
    inv_row[x] = jnp.transpose(inv_wide)[0:1, :]
    rowacc[...] = jnp.zeros_like(rowacc)

    near = places - 1 + NX - 1 + 1 + ny - 1

    @pl.when(x == y)
    def _():
        pl.semaphore_wait(barrier, near)

    @pl.when(x != y)
    def _():
        pl.semaphore_wait(barrier, near + 1)

    def kvx_copy(i):
        return remote(
            kv_send.at[(x + i) % NX], kv.at[:, z, x], kvx_sem.at[0], kvx_sem.at[1], at_x(i)
        )

    def inv_copy(i):
        return remote(inv_row.at[x], inv_row.at[x], inv_sem.at[0], inv_sem.at[1], at_x(i))

    def in_copies(g, i):
        cols = columns(((x + i) % NX) * groups + g)
        return (
            remote(q_hbm.at[:, cols], qin.at[g, x, 0], in_send, in_recv.at[g, x], at_x(i)),
            remote(do_hbm.at[:, cols], qin.at[g, x, 1], in_send, in_recv.at[g, x], at_x(i)),
        )

    def out_copies(g, i):
        head = x * groups + g
        to = (x + i) % NX
        return (
            remote(o_send.at[g, to, 0], att.at[:, columns(head)], o_send_sem, o_recv, at_x(i)),
            remote(o_send.at[g, to, 1], dqin.at[head], dq_send_sem, dq_recv.at[g], at_x(i)),
        )

    def z_copy(g, zz, up):
        chunk = kv.at[g, zz]
        send = zu_send if up else zd_send
        return remote(
            chunk, chunk, send.at[zz], z_recv.at[g, zz], at_z(1) if up else at_z(nz - 1)
        )

    def settle_recv(ref, sem):
        remote(ref, ref, sem, sem, at_x(1)).wait_recv()

    def settle_send(ref, sem):
        remote(ref, ref, sem, sem, at_x(1)).wait_send()

    for i in range(1, NX):
        kvx_copy(i).start()

    def in_sends(g):
        for i in range(1, NX):
            for copy in in_copies(g, i):
                copy.start()

    in_sends(0)
    for i in range(1, NX):
        inv_copy(i).start()

    def gain_copy(src, first, count, stage, target):
        dst = gains.at[pl.ds(first, count)]
        return remote(
            dst if src is None else src, dst, gain_sem.at[stage], gain_sem.at[3 + stage], target
        )

    gain_turn = gain_copy(own_gains, low * dev_heads, dev_heads, 0, (owner_row, y * nz + z))
    gain_core = gain_copy(None, low * dev_heads, dev_heads, 1, other_core)
    gain_half = gain_copy(None, half * 2 * dev_heads, 2 * dev_heads, 2, other_half)

    @pl.when(x != y)
    def _():
        gain_turn.start()

    @pl.when(x == y)
    def _():
        gains[pl.ds(low * dev_heads, dev_heads)] = own_gains[...]

    in_sends(1)
    @pl.loop(0, groups)
    def _(g):
        cols = columns(x * groups + g)
        pltpu.make_async_copy(q_hbm.at[:, cols], qin.at[g, x, 0], own_sem).start()
        pltpu.make_async_copy(do_hbm.at[:, cols], qin.at[g, x, 1], own_sem).start()

    index = lax.broadcasted_iota(jnp.int32, (1, text), 1)
    chunk_rows = NX * depth
    token = ((index // depth) % NX * nz + index // chunk_rows) * depth + index % depth
    bias = jnp.where(token < len_ref[0], 0.0, MASKED).astype(F32)
    scale = DH**-0.5
    nt = (((1,), (1,)), ((), ()))

    def compute(g):
        head = x * groups + g
        gain_q = gains[g, 0:1]
        gain_k = gains[g, 1:2]
        factor = gain_q * gain_k * (scale * LOG2E)
        column = jnp.zeros((1, DH), F32)
        keys = kv[g, :, :, 0].reshape(text, DH)
        values = kv[g, :, :, 1].reshape(text, DH)
        for i in (1, 2, 3, 0):
            source = (x + i) % NX
            q_unit = qin[g, source, 0].astype(F32) * inv[source]
            q_low = (q_unit * factor).astype(BF16)
            cot = qin[g, source, 1]
            sc = lax.dot_general(q_low, keys, nt, preferred_element_type=F32) + bias
            e = jnp.exp2(sc - jnp.max(sc, axis=-1, keepdims=True))
            inv_sum = 1.0 / jnp.sum(e, axis=-1, keepdims=True)
            o = jnp.dot(e.astype(BF16), values, preferred_element_type=F32) * inv_sum
            o_low = o.astype(BF16)
            delta = jnp.sum(cot.astype(F32) * o_low.astype(F32), axis=-1, keepdims=True)
            dp = lax.dot_general(cot, values, nt, preferred_element_type=F32)
            ds = (e * (dp - delta)).astype(BF16)
            dq = jnp.dot(ds, keys, preferred_element_type=F32) * inv_sum * gain_k
            column = column + jnp.sum(dq * q_unit, axis=0, keepdims=True)
            dq = dq * (gain_q * scale)
            if i == 0:
                att[:, columns(head)] = o_low
                dqin[head] = dq.astype(BF16)
            else:
                o_send[g, source, 0] = o_low
                o_send[g, source, 1] = dq.astype(BF16)
                for copy in out_copies(g, i):
                    copy.start()
        gain_row = g // dev_heads
        part[(gain_row % 2 * 2 + gain_row // 2) * dev_heads + g % dev_heads] = column * scale

    def post(g):
        settle_recv(dqin.at[pl.ds(0, NX - 1)], dq_recv.at[g])
        for xx in range(NX):
            head = xx * groups + g
            q_unit = q[:, columns(head)].astype(F32) * inv[x]
            rowacc[...] += dqin[head].astype(F32) * q_unit

    last = nz - 1

    def own_sends(g):
        @pl.when(z < last)
        def _():
            z_copy(g, z, True).start()

        @pl.when(z > 0)
        def _():
            z_copy(g, z, False).start()

    def step(n, carry):
        @pl.when(n == 0)
        def _():
            settle_recv(kv.at[:, z, 0 : NX - 1], kvx_sem.at[1])

            for g in range(AHEAD):
                own_sends(g)

        @pl.when(n + AHEAD < groups)
        def _():
            own_sends(n + AHEAD)

        @pl.loop(1, nz)
        def _(d):
            g = n - d
            live = jnp.logical_and(g >= 0, g < groups)

            @pl.when(jnp.logical_and(live, z - d >= 0))
            def _():
                z_copy(g, z - d, True).wait_recv()

                @pl.when(z < last)
                def _():
                    z_copy(g, z - d, True).start()

            @pl.when(jnp.logical_and(live, z + d < nz))
            def _():
                z_copy(g, z + d, False).wait_recv()

                @pl.when(z > 0)
                def _():
                    z_copy(g, z + d, False).start()

        @pl.when(n + 2 < groups)
        def _():
            in_sends(n + 2)

        @pl.when(n == min(2, last - 1))
        def _():
            @pl.when(x != y)
            def _():
                gain_turn.wait_recv()

            gain_core.start()
            settle_recv(inv_row.at[pl.ds(0, NX - 1)], inv_sem.at[1])
            for i in range(1, NX):
                source = (x + i) % NX
                wide = jnp.broadcast_to(inv_row[source], (DH, rows))
                inv[source] = jnp.transpose(wide)[:, 0:DH]
            pltpu.make_async_copy(qin.at[:, x], qin.at[:, x], own_sem).wait()

        @pl.when(n == min(3, last - 1))
        def _():
            gain_core.wait_recv()
            gain_half.start()

        @pl.when(n == last - 1)
        def _():
            gain_half.wait_recv()

        done = n - last

        @pl.when(jnp.logical_and(done >= 0, done < groups))
        def _():
            for i in range(1, NX):
                source = (x + i) % NX
                settle_recv(qin.at[done, source], in_recv.at[done, source])
            compute(done)

        return carry

    lax.fori_loop(0, groups + last, step, 0)

    span = 2 * dev_heads
    to_core = remote(
        part.at[pl.ds((1 - core) * span, span)], sum_c, sum_sem.at[0], sum_sem.at[1], other_core
    )
    to_core.start()
    to_core.wait_recv()
    core_part[...] = part[pl.ds(core * span, span)] + sum_c[...]

    def to_row(i):
        return remote(
            core_part,
            sum_y.at[y],
            sum_sem.at[2],
            sum_sem.at[3],
            (owner_row, (x + i) % NX * nz + z),
        )

    for i in range(1, NX):
        to_row(i).start()

    @pl.when(x != y)
    def _():
        to_row(0).start()

    @pl.when(x == y)
    def _():
        sum_y[y] = core_part[...]

    @pl.loop(0, groups - 2)
    def _(g):
        post(g)

    @pl.when(x == y)
    def _():
        settle_recv(sum_y.at[pl.ds(0, ny - 1)], sum_sem.at[3])

    @pl.when(x != y)
    def _():
        settle_recv(sum_y.at[pl.ds(0, ny)], sum_sem.at[3])

    total = sum_y[0]
    for i in range(1, ny):
        total = total + sum_y[i]
    z_part[...] = total

    def to_place(i):
        to = (place + i) % places
        return remote(
            z_part.at[pl.ds(to // nz * dev_heads, dev_heads)],
            sum_z.at[place],
            sum_sem.at[4],
            sum_sem.at[5],
            at_place(i),
        )

    @pl.loop(0, places - 1)
    def _(i):
        to_place((i + places // 4) % (places - 1) + 1).start()

    sum_z[place] = z_part[pl.ds(half * dev_heads, dev_heads)]
    post(groups - 2)
    post(groups - 1)
    row_mean = jnp.sum(rowacc[...], axis=-1, keepdims=True) * (1.0 / (heads * DH))
    slope = inv[x] * inv[x] * row_mean

    @pl.loop(0, heads)
    def _(head):
        result = inv[x] * dqin[head].astype(F32) - q[:, columns(head)].astype(F32) * slope
        grad[:, columns(head)] = result.astype(BF16)

    settle_recv(att.at[:, 0 : (NX - 1) * wx], o_recv)
    settle_send(kv_send.at[0 : NX - 1], kvx_sem.at[0])
    settle_send(qin.at[:, 0 : NX - 1], in_send)
    settle_send(o_send.at[:, 0 : NX - 1, 0], o_send_sem)
    settle_send(o_send.at[:, 0 : NX - 1, 1], dq_send_sem)
    settle_send(inv_row.at[pl.ds(0, NX - 1)], inv_sem.at[0])
    gain_core.wait_send()
    gain_half.wait_send()
    to_core.wait_send()

    @pl.when(x == y)
    def _():
        settle_send(sum_y.at[pl.ds(0, NX - 1)], sum_sem.at[2])

    @pl.when(x != y)
    def _():
        gain_turn.wait_send()
        settle_send(sum_y.at[pl.ds(0, NX)], sum_sem.at[2])

    @pl.loop(0, nz)
    def _(zz):
        @pl.when(jnp.logical_and(z < last, zz <= z))
        def _():
            settle_send(kv.at[:, zz], zu_send.at[zz])

        @pl.when(jnp.logical_and(z > 0, zz >= z))
        def _():
            settle_send(kv.at[:, zz], zd_send.at[zz])

    settle_recv(sum_z.at[pl.ds(0, places - 1)], sum_sem.at[5])
    total = sum_z[0]
    for i in range(1, places):
        total = total + sum_z[i]
    gg_ref[...] = total
    settle_send(sum_z.at[pl.ds(0, places - 1)], sum_sem.at[4])


def on_device(nz, nf, query_raw, out_cotangent, text_keys, text_values, text_lengths, gain_query, gain_key):
    rows, width = query_raw.shape[1:]
    depth = text_keys.shape[1]
    heads = width // DH
    text = depth * NX * nz
    own = heads // NX
    dev_heads = heads // nf
    ny = nf // NL
    dims = (nz, nf, heads, rows, text)
    any_space = pl.BlockSpec(memory_space=pl.ANY)
    vmem = pl.BlockSpec(memory_space=pltpu.VMEM)
    dma = pltpu.SemaphoreType.DMA
    attention, query_grad, gain_grad = pl.pallas_call(
        functools.partial(attention_kernel, dims),
        out_shape=(
            jax.ShapeDtypeStruct((rows, width), BF16),
            jax.ShapeDtypeStruct((rows, width), BF16),
            jax.ShapeDtypeStruct((dev_heads, 1, DH), F32),
        ),
        in_specs=[pl.BlockSpec(memory_space=pltpu.SMEM)] + [any_space] * 4 + [vmem] * 2,
        out_specs=(vmem, vmem, vmem),
        scratch_shapes=[
            pltpu.VMEM((own, nz, NX, 2, depth, DH), BF16),
            pltpu.VMEM((NX, own, 2, depth, DH), BF16),
            pltpu.VMEM((depth, width), BF16),
            pltpu.VMEM((depth, width), BF16),
            pltpu.VMEM((rows, width), BF16),
            pltpu.VMEM((own, NX, 2, rows, DH), BF16),
            pltpu.VMEM((own, NX, 2, rows, DH), BF16),
            pltpu.VMEM((heads, rows, DH), BF16),
            pltpu.VMEM((NX, 1, rows), F32),
            pltpu.VMEM((NX, rows, DH), F32),
            pltpu.VMEM((rows, DH), F32),
            pltpu.VMEM((dev_heads, 2, DH), F32),
            pltpu.VMEM((own, 2, DH), F32),
            pltpu.VMEM((own, 1, DH), F32),
            pltpu.VMEM((own // 2, 1, DH), F32),
            pltpu.VMEM((own // 2, 1, DH), F32),
            pltpu.VMEM((ny, own // 2, 1, DH), F32),
            pltpu.VMEM((own // 2, 1, DH), F32),
            pltpu.VMEM((NL // 2 * nz, dev_heads, 1, DH), F32),
            dma((3,)),
            dma,
            dma((2,)),
            dma((own, nz)),
            dma((nz,)),
            dma((nz,)),
            dma,
            dma((own, NX)),
            dma,
            dma,
            dma,
            dma((own,)),
            dma((2,)),
            dma((6,)),
            dma((6,)),
        ],
        compiler_params=pltpu.CompilerParams(
            collective_id=0, has_side_effects=True, vmem_limit_bytes=VMEM_LIMIT
        ),
    )(
        text_lengths,
        query_raw[0],
        out_cotangent[0],
        text_keys[0],
        text_values[0],
        gain_query.reshape(dev_heads, 1, DH),
        gain_key.reshape(dev_heads, 1, DH),
    )
    return attention[None], query_grad[None], gain_grad.reshape(dev_heads * DH)


def solution(mesh):
    nf, ns = mesh.shape["fsdp"], mesh.shape["seq"]
    tokens = P("fsdp", "seq", None)
    return jax.shard_map(
        functools.partial(on_device, ns // NX, nf),
        mesh=mesh,
        in_specs=(tokens, tokens, tokens, tokens, P("fsdp"), P("fsdp"), P("fsdp")),
        out_specs=(tokens, tokens, P("fsdp")),
        check_vma=False,
    )
```
